256 devices in a mesh: dom: 8 (over x, z_lo), tx: 4 (over z_hi), ty: 8 (over y, core).
Axes of the slice: x: 4, y: 4, z: 8 (z_hi: 4, z_lo: 2; z = z_hi * 2 + z_lo), core: 2. Of those that a mesh axis runs over, the one named last changes fastest.
Arguments:
- ensemble: float32 [128, 32, 2048], P('dom', 'tx', 'ty'), may hold values from -9 to 9
- diffusivity: float32 [32, 2048], P('tx', 'ty'), may hold values from 0.02 to 0.09
- velocity: float32 [3, 32, 2048], P(None, 'tx', 'ty'), may hold values from 0.05 to 0.15
- observed: float32 [32, 2048], P('tx', 'ty'), may hold values from -24 to 24
- obs_weight: float32 [32, 2048], P('tx', 'ty'), may hold values from 0.03 to 2.8, as said below
- noise: float32 [2, 128, 128], P(None, None, 'dom'), may hold values from -6 to 6
Outputs:
- updated: float32 [128, 32, 2048], P('dom', 'tx', 'ty')
The draws below stay inside these ranges and needn't reach their ends.
Inputs may be any that keep to these rules, and one draw needn't show every extreme that they name: obs_weight is positive.
All inputs are finite; a program needn't handle non-finite values.
Results may differ from the reference program's by a relative error of at most 0.00016.
Values sent between devices are 32-bit elements; how exact they have to be, the bound alone decides.
A program may use at most 64 MiB of HBM per device.

```python
import math
import jax
import jax.numpy as jnp
from jax import lax

NZ = 32
ITERS = 2
PARTICLES = 128
NX = 32
NY = 64
CELLS = 65536


def draw_obs_weight(key, part):
    position = jnp.arange(NX, dtype=jnp.float32)[:, None] / NX
    rough = jax.random.uniform(key, (NX, NY * NZ), jnp.float32, -1.1, 1.1)
    return 0.1 * jnp.exp(math.log(9.0) * position + rough)


def block_levels(own_key, dims, split, smallest, largest):
    def one(dim, shards_of):
        draws = jax.random.uniform(jax.random.fold_in(jax.random.fold_in(own_key, 6), dim), (shards_of,), jnp.float32, smallest / len(split), largest / len(split))
        return jnp.repeat(jnp.exp(draws), dims[dim] // shards_of).reshape((-1,) + (1,) * (len(dims) - dim - 1))

    gain = one(*split[0])
    for cut in split[1:]:
        gain = gain * one(*cut)
    return gain


def centred(rng, shape, scale, limit, split=(), kind=jnp.bfloat16):
    values = jax.random.normal(rng, shape, jnp.float32) * scale
    if len(split) > 0:
        values = block_levels(rng, shape, split, -0.22, 0.18) * values
    return jnp.clip(values, min=-limit, max=limit).astype(kind)


def setup_inputs(seed: int = 0) -> dict:
    seeds = jax.random.split(jax.random.key(seed), 7)
    ensemble = centred(seeds[0], (PARTICLES, NX, NY * NZ), 1.5, 9.0, ((0, 8), (1, 4), (2, 8)), jnp.float32)
    diffusivity = jnp.clip(jnp.exp(math.log(0.09) - 1.50407746 * jax.random.uniform(seeds[1], (NX, NY * NZ), jnp.float32) ** block_levels(seeds[1], (NX, NY * NZ), ((0, 4), (1, 8)), -0.2, 0.2)), 0.02, 0.09)
    velocity = jnp.clip(jnp.exp(math.log(0.15) - 1.0986123 * jax.random.uniform(seeds[2], (3, NX, NY * NZ), jnp.float32) ** block_levels(seeds[2], (3, NX, NY * NZ), ((1, 4), (2, 8)), -0.2, 0.2)), 0.05, 0.15)
    observed = centred(seeds[3], (NX, NY * NZ), 4.0, 24.0, ((0, 4), (1, 8)), jnp.float32)
    obs_weight = draw_obs_weight(jax.random.fold_in(seeds[6], 71), 0)
    noise = centred(seeds[5], (ITERS, PARTICLES, PARTICLES), 1.0, 6.0, ((2, 8),), jnp.float32)
    return {"ensemble": ensemble, "diffusivity": diffusivity, "velocity": velocity, "observed": observed, "obs_weight": obs_weight, "noise": noise}


def neighbour_sum(padded):
    total = padded[:, :-2, 1:-1, 1:-1] + padded[:, 2:, 1:-1, 1:-1]
    total = total + padded[:, 1:-1, :-2, 1:-1] + padded[:, 1:-1, 2:, 1:-1]
    total = total + padded[:, 1:-1, 1:-1, :-2] + padded[:, 1:-1, 1:-1, 2:]
    return total

def pad_cells(values):
    return jnp.pad(values, ((0, 0), (1, 1), (1, 1), (1, 1)))

def advance(values, diffusion, speeds, centre):
    padded = pad_cells(values)
    result = centre * values + diffusion * neighbour_sum(padded)
    result = result + speeds[0] * padded[:, :-2, 1:-1, 1:-1]
    result = result + speeds[1] * padded[:, 1:-1, :-2, 1:-1]
    return result + speeds[2] * padded[:, 1:-1, 1:-1, :-2]

def retreat(adjoint, diffusion, speeds, centre):
    spread = pad_cells(diffusion * adjoint)
    carry_x = pad_cells(speeds[0] * adjoint)
    carry_y = pad_cells(speeds[1] * adjoint)
    carry_z = pad_cells(speeds[2] * adjoint)
    result = centre * adjoint + neighbour_sum(spread)
    result = result + carry_x[:, 2:, 1:-1, 1:-1] + carry_y[:, 1:-1, 2:, 1:-1]
    return result + carry_z[:, 1:-1, 1:-1, 2:]

def reference(ensemble, diffusivity, velocity, observed, obs_weight, noise):
    shape_full = (PARTICLES, NX, NY, NZ)
    state = ensemble.reshape(shape_full)
    diffusion = diffusivity.reshape(NX, NY, NZ)
    speeds = velocity.reshape(3, NX, NY, NZ)
    target = observed.reshape(NX, NY, NZ)
    weight = obs_weight.reshape(NX, NY, NZ)
    centre = 1.0 - 6.0 * diffusion - speeds[0] - speeds[1] - speeds[2]
    step_size = PARTICLES / (4.0 * CELLS)
    growth = step_size * (CELLS + 1) / PARTICLES
    drift = step_size / PARTICLES
    spread_scale = math.sqrt(2.0 * step_size / PARTICLES)
    for iteration in range(ITERS):
        images = advance(advance(state, diffusion, speeds, centre), diffusion, speeds, centre)
        residual = weight * (images - target)
        gradient = retreat(retreat(residual, diffusion, speeds, centre), diffusion, speeds, centre) + state
        mean = lax.optimization_barrier(jnp.mean(state, axis=0))
        anomaly = state - mean
        flat_anomaly = anomaly.reshape(PARTICLES, -1)
        flat_gradient = gradient.reshape(PARTICLES, -1)
        gram = jnp.dot(flat_anomaly, flat_gradient.T, precision=lax.Precision.HIGHEST, preferred_element_type=jnp.float32)
        mixing = -drift * gram + spread_scale * noise[iteration]
        moved = jnp.dot(mixing.T, flat_anomaly, precision=lax.Precision.HIGHEST, preferred_element_type=jnp.float32)
        state = state + growth * anomaly + moved.reshape(shape_full)
    return state.reshape(PARTICLES, NX, NY * NZ)
```

```python
import functools
import itertools
import math

import jax
import jax.numpy as jnp
from jax import lax
from jax.experimental import pallas as pl
from jax.experimental.pallas import tpu as pltpu
from jax.sharding import PartitionSpec as P

NZ = 32
MESH = pl.DeviceIdType.MESH
LANES = 128
COEFS = 8


def dot(a, b, dims):
    return lax.dot_general(
        a,
        b,
        (dims, ((), ())),
        precision=lax.Precision.HIGHEST,
        preferred_element_type=jnp.float32,
    )


def step_row(here, west, east, coefs, tiles):
    lane = lax.broadcasted_iota(jnp.int32, (1, LANES), 1)
    depth = lane % NZ
    up = [pltpu.roll(tile, NZ, 1) for tile in here]
    down = [pltpu.roll(tile, LANES - NZ, 1) for tile in here]
    out = []
    for k in range(tiles):
        diffusion, vx, vy, vz = (coefs[k][i : i + 1] for i in range(4))
        centre = 1.0 - 6.0 * diffusion - vx - vy - vz
        south = jnp.where(lane < NZ, up[(k + 2) % 3], up[k])
        north = jnp.where(lane >= LANES - NZ, down[(k + 1) % 3], down[k])
        below = pltpu.roll(here[k], 1, 1)
        above = pltpu.roll(here[k], LANES - 1, 1)
        result = centre * here[k] + diffusion * (east[k] + north)
        result = result + (diffusion + vx) * west[k] + (diffusion + vy) * south
        result = result + jnp.where(depth > 0, diffusion + vz, 0.0) * below
        result = result + jnp.where(depth < NZ - 1, diffusion, 0.0) * above
        out.append(result)
    return out


def kernel(
    sizes, consts,
    ens, dif, vel, obs, wgt, noi, out,
    XB, TB, YL, YR, CN, LB, YB, SA, YA, SF, OV, WV, NV, NT, NA, GP, RL, RB, AL, AB, GA, DV, OB,
    load, send, hrecv, recv, osem,
):
    nd, nt, ny, rows, mem, total = sizes
    growth, drift, spread = consts
    d, t, y = lax.axis_index("dom"), lax.axis_index("tx"), lax.axis_index("ty")
    chip_y, core = y // 2, lax.rem(y, 2)
    blk, quad = d * 2 + core, t * (ny // 2) + chip_y
    width = rows + 4

    def at(dd, tt, yy):
        return (lax.rem(d + dd, nd), lax.rem(t + tt, nt), lax.rem(y + yy, ny))

    dom_peers = [at(k, 0, 0) for k in range(1, nd)]
    dc_peers = []
    for k in range(1, 2 * nd):
        dc_peers.append((lax.rem(d + k // 2, nd), t, chip_y * 2 + lax.rem(core + k % 2, 2)))
    yt_peers = []
    for k in range(1, nt * (ny // 2)):
        a, b = k // (ny // 2), k % (ny // 2)
        yt_peers.append((d, lax.rem(t + a, nt), lax.rem(chip_y + b, ny // 2) * 2 + core))
    halo_peers = {}
    for a, b in itertools.product((-1, 0, 1), (-1, 0, 1)):
        if a or b:
            halo_peers[(a, b)] = at(0, a % nt, b % ny)

    loads = [
        pltpu.make_async_copy(dif, XB.at[pl.ds(2, rows), mem], load.at[0]),
        pltpu.make_async_copy(obs, OV, load.at[1]),
        pltpu.make_async_copy(wgt, WV, load.at[2]),
        pltpu.make_async_copy(noi, NV, load.at[3]),
    ]
    for k in range(3):
        loads.append(
            pltpu.make_async_copy(vel.at[k], XB.at[pl.ds(2, rows), mem + 1 + k], load.at[4 + k])
        )
    for x in range(rows):
        loads.append(
            pltpu.make_async_copy(ens.at[:, x], XB.at[2 + x, pl.ds(0, mem)], load.at[7 + x])
        )
    for copy in loads:
        copy.start()

    barrier = pltpu.get_barrier_semaphore()
    greeted = dc_peers + yt_peers + list(halo_peers.values())
    for peer in greeted:
        pl.semaphore_signal(barrier, inc=1, device_id=peer, device_id_type=MESH)
    zero = jnp.zeros((1,) + TB.shape[1:], jnp.float32)
    TB[0:1] = zero
    TB[width - 1 : width] = zero
    for copy in loads:
        copy.wait()
    NT[...] = NV[0].T
    pl.semaphore_wait(barrier, len(greeted))

    def remote(src, dst, ss, rs, peer):
        copy = pltpu.make_async_remote_copy(
            src_ref=src, dst_ref=dst, send_sem=ss, recv_sem=rs, device_id=peer, device_id_type=MESH
        )
        copy.start()
        return copy

    left, right = pl.ds(0, LANES), pl.ds(LANES, LANES)
    own, body = pl.ds(0, mem), pl.ds(2, rows)
    halos = []
    for i, (key, src, dst) in enumerate(
        (
            ((1, 0), XB.at[pl.ds(rows, 2)], XB.at[pl.ds(0, 2)]),
            ((-1, 0), XB.at[pl.ds(2, 2)], XB.at[pl.ds(rows + 2, 2)]),
            ((0, 1), XB.at[body, :, right], YL),
            ((0, -1), XB.at[body, :, left], YR),
            ((1, 1), XB.at[rows + 1, own, right], CN.at[0]),
            ((1, -1), XB.at[rows + 1, own, left], CN.at[1]),
            ((-1, 1), XB.at[2, own, right], CN.at[2]),
            ((-1, -1), XB.at[2, own, left], CN.at[3]),
        )
    ):
        halos.append(remote(src, dst, send.at[6 + i], hrecv.at[i], halo_peers[key]))
    for k, peer in enumerate(dom_peers):
        remote(XB.at[2 + peer[0], own], SA.at[d], send.at[0], recv.at[0], peer)
    for k, peer in enumerate(dom_peers):
        remote(NT, NA.at[d], send.at[1], recv.at[1], peer)
    keep = pltpu.make_async_copy(XB.at[body, own], SF.at[d], load.at[0])
    keep.start()
    SA[d] = XB[2 + d, 0:mem]
    NA[d] = NT[...]
    for copy in halos:
        copy.wait_recv()

    @pl.when(t == 0)
    def _():
        XB[0:2] = jnp.zeros((2,) + XB.shape[1:], jnp.float32)

    @pl.when(t == nt - 1)
    def _():
        XB[rows + 2 : rows + 4] = jnp.zeros((2,) + XB.shape[1:], jnp.float32)

    has_left = (y > 0).astype(jnp.float32)
    has_right = (y < ny - 1).astype(jnp.float32)
    has_west = (t > 0).astype(jnp.float32)
    has_east = (t < nt - 1).astype(jnp.float32)
    is_right = lax.broadcasted_iota(jnp.int32, (1, LANES), 1) < LANES // 2
    TB[2 : rows + 2] = jnp.where(is_right[None], YR[...] * has_right, YL[...] * has_left)
    TB[1, 0:mem] = jnp.where(is_right, CN[1] * has_right, CN[0] * has_left) * has_west
    TB[rows + 2, 0:mem] = jnp.where(is_right, CN[3] * has_right, CN[2] * has_left) * has_east
    TB[1, mem:] = zero[0, mem:]
    TB[rows + 2, mem:] = zero[0, mem:]

    def tiles_of(r):
        return [XB[r, 0:mem, 0:LANES], XB[r, 0:mem, LANES:], TB[r, 0:mem]]

    def first(r, carry):
        coefs = [XB[r, mem:, 0:LANES], XB[r, mem:, LANES:], TB[r, mem:]]
        found = step_row(tiles_of(r), tiles_of(r - 1), tiles_of(r + 1), coefs, 3)
        for k in range(3):
            LB[r - 1, :, k * LANES : (k + 1) * LANES] = found[k]
        return carry

    lax.fori_loop(1, rows + 3, first, 0)

    def second(r, carry):
        coefs = [XB[r + 2, mem:, 0:LANES], XB[r + 2, mem:, LANES:]]
        mid, before, after = (
            [LB[s, :, k * LANES : (k + 1) * LANES] for k in range(3)] for s in (r + 1, r, r + 2)
        )
        found = step_row(mid, before, after, coefs, 2)
        for k in range(2):
            YB[r, :, k * LANES : (k + 1) * LANES] = found[k]
        return carry

    lax.fori_loop(0, rows, second, 0)

    for peer in dom_peers:
        remote(YB.at[peer[0]], YA.at[d], send.at[2], recv.at[2], peer)
    for peer in dom_peers:
        remote(XB.at[body, own], SF.at[d], send.at[14], recv.at[6], peer)
    YA[d] = YB[d]

    def wait_all(ref, count, sem):
        part = ref.at[pl.ds(0, count)]
        pltpu.make_async_copy(part, part, sem).wait()

    wait_all(SA, nd - 1, recv.at[0])
    cells = rows * 0 + SA.shape[2]
    state = SA[...].reshape(total, cells)
    anomaly = state - jnp.sum(state, axis=0, keepdims=True) * (1.0 / total)
    near = dot(state, anomaly, ((1,), (1,)))
    target, weight = OV[pl.ds(d, 1)], WV[pl.ds(d, 1)]
    wait_all(YA, nd - 1, recv.at[2])
    image = YA[...].reshape(total, cells)
    centred = weight * (image - jnp.sum(image, axis=0, keepdims=True) * (1.0 / total))
    gram = near + dot(image - target, centred, ((1,), (1,)))
    GP[...] = gram.reshape(GP.shape)

    for peer in dc_peers:
        theirs = peer[0] * 2 + lax.rem(peer[2], 2)
        remote(GP.at[theirs], RL.at[blk], send.at[3], recv.at[3], peer)
    RL[blk] = GP[blk]
    wait_all(RL, 2 * nd - 1, recv.at[3])
    RB[...] = jnp.sum(RL[...], axis=0)
    for peer in yt_peers:
        remote(RB, AL.at[quad], send.at[4], recv.at[4], peer)
    AL[quad] = RB[...]
    wait_all(AL, len(yt_peers), recv.at[4])
    AB[...] = jnp.sum(AL[...], axis=0)
    for peer in dc_peers:
        remote(AB, GA.at[blk], send.at[5], recv.at[5], peer)
    GA[blk] = AB[...]
    wait_all(NA, nd - 1, recv.at[1])
    mine = spread * NV[1].T
    wait_all(GA, 2 * nd - 1, recv.at[5])

    gram = GA[...].reshape(total, total)
    noise = NA[...].reshape(total, total)
    eye = (
        lax.broadcasted_iota(jnp.int32, (total, total), 0)
        == lax.broadcasted_iota(jnp.int32, (total, total), 1)
    ).astype(jnp.float32)
    moved = (1.0 + growth) * eye + (spread * noise - drift * gram)
    DV[...] = moved.reshape(DV.shape)
    column = jnp.sum(moved, axis=0, keepdims=True) * (1.0 / total)
    spans = moved - column
    moved_own = DV[d]
    weights = moved_own - jnp.sum(moved_own, axis=1, keepdims=True) * (1.0 / total) + 1.0 / total
    later = dot(dot(weights, gram, ((1,), (0,))), spans, ((1,), (1,)))
    mixing = mine - drift * later
    last = moved_own + growth * (moved_own - column) + dot(mixing, spans, ((1,), (0,)))
    last = last - jnp.sum(last, axis=1, keepdims=True) * (1.0 / total) + 1.0 / total

    keep.wait()
    wait_all(SF, nd - 1, recv.at[6])
    stores = []
    for x in range(rows):
        OB[x] = dot(last, SF[:, x].reshape(total, cells), ((1,), (0,)))
        store = pltpu.make_async_copy(OB.at[x], out.at[:, x], osem.at[x])
        store.start()
        stores.append(store)

    for copy in halos:
        copy.wait_send()
    wait_all(SA, nd - 1, send.at[0])
    wait_all(NA, nd - 1, send.at[1])
    wait_all(YA, nd - 1, send.at[2])
    wait_all(RL, 2 * nd - 1, send.at[3])
    wait_all(AL, len(yt_peers), send.at[4])
    wait_all(GA, 2 * nd - 1, send.at[5])
    wait_all(SF, nd - 1, send.at[14])
    for store in stores:
        store.wait()


def on_device(ensemble, diffusivity, velocity, observed, obs_weight, noise):
    nd, nt, ny = (lax.axis_size(a) for a in ("dom", "tx", "ty"))
    mem, rows, cells = ensemble.shape
    total = mem * nd
    iters = noise.shape[0]
    cell_count = rows * nt * cells * ny
    step_size = total / (4.0 * cell_count)
    growth = step_size * (cell_count + 1) / total
    drift = step_size / total
    spread = math.sqrt(2.0 * step_size / total)
    f32 = functools.partial(pltpu.VMEM, dtype=jnp.float32)
    high = mem + COEFS
    half = mem // 2
    quads = nt * (ny // 2)
    scratch = [
        f32((rows + 4, high, cells)),
        f32((rows + 4, high, LANES)),
        f32((rows, high, LANES)),
        f32((rows, high, LANES)),
        f32((4, mem, LANES)),
        f32((rows + 2, mem, cells + LANES)),
        f32((rows, mem, cells)),
        f32((nd, mem, cells)),
        f32((nd, mem, cells)),
        f32((nd, rows, mem, cells)),
        f32((rows, cells)),
        f32((rows, cells)),
        f32(noise.shape),
        f32((mem, total)),
        f32((nd, mem, total)),
        f32((2 * nd, half, total)),
        f32((2 * nd, half, total)),
        f32((half, total)),
        f32((quads, half, total)),
        f32((half, total)),
        f32((2 * nd, half, total)),
        f32((nd, mem, total)),
        f32((rows, mem, cells)),
        pltpu.SemaphoreType.DMA((7 + rows,)),
        pltpu.SemaphoreType.DMA((15,)),
        pltpu.SemaphoreType.DMA((8,)),
        pltpu.SemaphoreType.DMA((7,)),
        pltpu.SemaphoreType.DMA((rows,)),
    ]
    anywhere = pl.BlockSpec(memory_space=pl.ANY)
    return pl.pallas_call(
        functools.partial(kernel, (nd, nt, ny, rows, mem, total), (growth, drift, spread)),
        out_shape=jax.ShapeDtypeStruct(ensemble.shape, jnp.float32),
        in_specs=[anywhere] * 6,
        out_specs=anywhere,
        scratch_shapes=scratch,
        compiler_params=pltpu.CompilerParams(
            collective_id=0, has_side_effects=True, vmem_limit_bytes=32 * 2**20
        ),
        name="langevin",
    )(ensemble, diffusivity, velocity, observed, obs_weight, noise)


def solution(mesh):
    return jax.shard_map(
        on_device,
        mesh=mesh,
        in_specs=(
            P("dom", "tx", "ty"),
            P("tx", "ty"),
            P(None, "tx", "ty"),
            P("tx", "ty"),
            P("tx", "ty"),
            P(None, None, "dom"),
        ),
        out_specs=P("dom", "tx", "ty"),
        check_vma=False,
    )
```

```python
import functools
import itertools
import math

import jax
import jax.numpy as jnp
from jax import lax
from jax.experimental import pallas as pl
from jax.experimental.pallas import tpu as pltpu
from jax.sharding import PartitionSpec as P

NZ = 32
MESH = pl.DeviceIdType.MESH
LANES = 128
COEFS = 8
WINDOWS = (3, 0, 2, 3)


def dot(a, b, dims):
    return lax.dot_general(
        a,
        b,
        (dims, ((), ())),
        precision=lax.Precision.HIGHEST,
        preferred_element_type=jnp.float32,
    )


def step_row(here, west, east, coefs, tiles):
    lane = lax.broadcasted_iota(jnp.int32, (1, LANES), 1)
    depth = lane % NZ
    up = [pltpu.roll(tile, NZ, 1) for tile in here]
    down = [pltpu.roll(tile, LANES - NZ, 1) for tile in here]
    out = []
    for k in range(tiles):
        diffusion, vx, vy, vz = (coefs[k][i : i + 1] for i in range(4))
        centre = 1.0 - 6.0 * diffusion - vx - vy - vz
        south = jnp.where(lane < NZ, up[(k + 2) % 3], up[k])
        north = jnp.where(lane >= LANES - NZ, down[(k + 1) % 3], down[k])
        below = pltpu.roll(here[k], 1, 1)
        above = pltpu.roll(here[k], LANES - 1, 1)
        result = centre * here[k] + diffusion * (east[k] + north)
        result = result + (diffusion + vx) * west[k] + (diffusion + vy) * south
        result = result + jnp.where(depth > 0, diffusion + vz, 0.0) * below
        result = result + jnp.where(depth < NZ - 1, diffusion, 0.0) * above
        out.append(result)
    return out


def kernel(
    sizes, consts,
    ens, dif, vel, obs, wgt, noi, out,
    XB, TB, YL, YR, CN, LB, YB, SA, YA, SF, OV, WV, NV, NA, GP, RL, RB, AL, AB, GA, DV,
    load, send, hrecv, recv,
):
    nd, nt, ny, rows, mem, total = sizes
    growth, drift, spread = consts
    d, t, y = lax.axis_index("dom"), lax.axis_index("tx"), lax.axis_index("ty")
    chip_y, core = y // 2, lax.rem(y, 2)
    blk, quad = d * 2 + core, t * (ny // 2) + chip_y
    width = rows + 4

    def at(dd, tt, yy):
        return (lax.rem(d + dd, nd), lax.rem(t + tt, nt), lax.rem(y + yy, ny))

    dom_peers = [at(k, 0, 0) for k in range(1, nd)]
    dc_peers = []
    for k in range(1, 2 * nd):
        dc_peers.append((lax.rem(d + k // 2, nd), t, chip_y * 2 + lax.rem(core + k % 2, 2)))
    yt_peers = []
    for k in range(1, nt * (ny // 2)):
        a, b = k // (ny // 2), k % (ny // 2)
        yt_peers.append((d, lax.rem(t + a, nt), lax.rem(chip_y + b, ny // 2) * 2 + core))
    halo_peers = {}
    for a, b in itertools.product((-1, 0, 1), (-1, 0, 1)):
        if a or b:
            halo_peers[(a, b)] = at(0, a % nt, b % ny)

    barrier = pltpu.get_barrier_semaphore()
    greeted = [at(0, a % nt, b % ny) for a in (0, -1, 1) for b in (-2, -1, 0, 1, 2) if a or b]
    greeted += dom_peers
    for peer in greeted:
        pl.semaphore_signal(barrier, inc=1, device_id=peer, device_id_type=MESH)

    pending = {}

    def settle(name):
        pending.pop(name)()

    def finish():
        for name in list(pending):
            settle(name)


    loads = [pltpu.make_async_copy(dif, XB.at[pl.ds(2, rows), mem], load.at[0])]
    for k in range(3):
        loads.append(
            pltpu.make_async_copy(vel.at[k], XB.at[pl.ds(2, rows), mem + 1 + k], load.at[1 + k])
        )
    for x in range(rows):
        loads.append(
            pltpu.make_async_copy(ens.at[:, x], XB.at[2 + x, pl.ds(0, mem)], load.at[4 + x])
        )
    for copy in loads:
        copy.start()
    extras = [
        pltpu.make_async_copy(src, dst, load.at[4 + rows + k])
        for k, (src, dst) in enumerate(((obs, OV), (wgt, WV), (noi, NV)))
    ]
    for copy in extras:
        copy.start()
    zero = jnp.zeros((1,) + TB.shape[1:], jnp.float32)
    TB[0:1] = zero
    TB[width - 1 : width] = zero
    for copy in loads + extras:
        copy.wait()

    pl.semaphore_wait(barrier, len(greeted))

    def remote(src, dst, ss, rs, peer):
        copy = pltpu.make_async_remote_copy(
            src_ref=src, dst_ref=dst, send_sem=ss, recv_sem=rs, device_id=peer, device_id_type=MESH
        )
        copy.start()
        return copy

    left, right = pl.ds(0, LANES), pl.ds(LANES, LANES)
    own, body = pl.ds(0, mem), pl.ds(2, rows)
    halos = []
    for i, (key, src, dst) in enumerate(
        (
            ((1, 0), XB.at[pl.ds(rows, 2)], XB.at[pl.ds(0, 2)]),
            ((-1, 0), XB.at[pl.ds(2, 2)], XB.at[pl.ds(rows + 2, 2)]),
            ((0, 1), XB.at[body, :, right], YL),
            ((0, -1), XB.at[body, :, left], YR),
            ((1, 1), XB.at[rows + 1, own, right], CN.at[0]),
            ((1, -1), XB.at[rows + 1, own, left], CN.at[1]),
            ((-1, 1), XB.at[2, own, right], CN.at[2]),
            ((-1, -1), XB.at[2, own, left], CN.at[3]),
        )
    ):
        halos.append(remote(src, dst, send.at[6 + i], hrecv.at[i], halo_peers[key]))
    for k, peer in enumerate(dom_peers):
        remote(XB.at[2 + peer[0], own], SA.at[d], send.at[0], recv.at[0], peer)
    for k, peer in enumerate(dom_peers):
        remote(NV.at[0], NA.at[d], send.at[1], recv.at[1], peer)

    def wait_all(name, ref, count, sem):
        def wait():
            part = ref.at[pl.ds(0, count)]
            pltpu.make_async_copy(part, part, sem).wait()

        pending[name] = wait

    def bulk(window):
        begin, count = sum(WINDOWS[:window]), WINDOWS[window]
        if count:
            for peer in dom_peers:
                remote(
                    XB.at[pl.ds(2 + begin, count), own],
                    SF.at[d, pl.ds(begin, count)],
                    send.at[14 + window],
                    recv.at[6 + window],
                    peer,
                )
            slots = SF.at[:, pl.ds(begin, count)]
            wait_all(f"ensemble {window}", slots, nd - 1, recv.at[6 + window])
            wait_all(f"ensemble {window} sent", slots, nd - 1, send.at[14 + window])

    bulk(0)
    keep = pltpu.make_async_copy(XB.at[body, own], SF.at[d], load.at[7 + rows])
    keep.start()
    pending['keep'] = keep.wait
    SA[d] = XB[2 + d, 0:mem]
    NA[d] = NV[0]

    def wait_halos():
        for copy in halos:
            copy.wait_recv()

    def sent_halos():
        for copy in halos:
            copy.wait_send()

    pending["halos"] = wait_halos
    pending["halos sent"] = sent_halos
    wait_all("members", SA, nd - 1, recv.at[0])
    wait_all("members sent", SA, nd - 1, send.at[0])
    wait_all("noise", NA, nd - 1, recv.at[1])
    wait_all("noise sent", NA, nd - 1, send.at[1])
    settle("halos")

    @pl.when(t == 0)
    def _():
        XB[0:2] = jnp.zeros((2,) + XB.shape[1:], jnp.float32)

    @pl.when(t == nt - 1)
    def _():
        XB[rows + 2 : rows + 4] = jnp.zeros((2,) + XB.shape[1:], jnp.float32)

    has_left = (y > 0).astype(jnp.float32)
    has_right = (y < ny - 1).astype(jnp.float32)
    has_west = (t > 0).astype(jnp.float32)
    has_east = (t < nt - 1).astype(jnp.float32)
    is_right = lax.broadcasted_iota(jnp.int32, (1, LANES), 1) < LANES // 2
    TB[2 : rows + 2] = jnp.where(is_right[None], YR[...] * has_right, YL[...] * has_left)
    TB[1, 0:mem] = jnp.where(is_right, CN[1] * has_right, CN[0] * has_left) * has_west
    TB[rows + 2, 0:mem] = jnp.where(is_right, CN[3] * has_right, CN[2] * has_left) * has_east
    TB[1, mem:] = zero[0, mem:]
    TB[rows + 2, mem:] = zero[0, mem:]

    def tiles_of(r):
        return [XB[r, 0:mem, 0:LANES], XB[r, 0:mem, LANES:], TB[r, 0:mem]]

    def first(r, carry):
        coefs = [XB[r, mem:, 0:LANES], XB[r, mem:, LANES:], TB[r, mem:]]
        found = step_row(tiles_of(r), tiles_of(r - 1), tiles_of(r + 1), coefs, 3)
        for k in range(3):
            LB[r - 1, :, k * LANES : (k + 1) * LANES] = found[k]
        return carry

    lax.fori_loop(1, rows + 3, first, 0)

    def second(r, carry):
        coefs = [XB[r + 2, mem:, 0:LANES], XB[r + 2, mem:, LANES:]]
        mid, before, after = (
            [LB[s, :, k * LANES : (k + 1) * LANES] for k in range(3)] for s in (r + 1, r, r + 2)
        )
        found = step_row(mid, before, after, coefs, 2)
        for k in range(2):
            YB[r, :, k * LANES : (k + 1) * LANES] = found[k]
        return carry

    lax.fori_loop(0, rows, second, 0)

    for peer in dom_peers:
        remote(YB.at[peer[0]], YA.at[d], send.at[2], recv.at[2], peer)
    bulk(1)
    YA[d] = YB[d]
    wait_all("images", YA, nd - 1, recv.at[2])
    wait_all("images sent", YA, nd - 1, send.at[2])
    settle("members")
    cells = SA.shape[2]
    state = SA[...].reshape(total, cells)
    anomaly = state - jnp.sum(state, axis=0, keepdims=True) * (1.0 / total)
    near = dot(state, anomaly, ((1,), (1,)))
    target, weight = OV[pl.ds(d, 1)], WV[pl.ds(d, 1)]
    settle("images")
    image = YA[...].reshape(total, cells)
    centred = weight * (image - jnp.sum(image, axis=0, keepdims=True) * (1.0 / total))
    gram = near + dot(image - target, centred, ((1,), (1,)))
    GP[...] = gram.reshape(GP.shape)

    for peer in dc_peers:
        theirs = peer[0] * 2 + lax.rem(peer[2], 2)
        remote(GP.at[theirs], RL.at[blk], send.at[3], recv.at[3], peer)
    RL[blk] = GP[blk]
    wait_all("parts", RL, 2 * nd - 1, recv.at[3])
    wait_all("parts sent", RL, 2 * nd - 1, send.at[3])
    bulk(2)
    settle("parts")
    RB[...] = jnp.sum(RL[...], axis=0)
    for peer in yt_peers:
        remote(RB, AL.at[quad], send.at[4], recv.at[4], peer)
    AL[quad] = RB[...]
    wait_all("tiles", AL, len(yt_peers), recv.at[4])
    wait_all("tiles sent", AL, len(yt_peers), send.at[4])
    bulk(3)
    settle("tiles")
    AB[...] = jnp.sum(AL[...], axis=0)
    for peer in dc_peers:
        remote(AB, GA.at[blk], send.at[5], recv.at[5], peer)
    GA[blk] = AB[...]
    wait_all("blocks", GA, 2 * nd - 1, recv.at[5])
    wait_all("blocks sent", GA, 2 * nd - 1, send.at[5])
    settle("noise")
    mine = spread * NV[1]
    settle("blocks")

    gram = GA[...].reshape(total, total)
    noise = NA[...].reshape(total, total)
    eye = (
        lax.broadcasted_iota(jnp.int32, (total, total), 0)
        == lax.broadcasted_iota(jnp.int32, (total, total), 1)
    ).astype(jnp.float32)
    moved = (1.0 + growth) * eye + (spread * noise - drift * gram)
    DV[...] = moved.reshape(DV.shape)
    column = jnp.sum(moved, axis=0, keepdims=True) * (1.0 / total)
    spans = moved - column
    moved_own = DV[d]
    weights = moved_own - jnp.sum(moved_own, axis=1, keepdims=True) * (1.0 / total) + 1.0 / total
    later = dot(dot(weights, gram, ((1,), (0,))), spans, ((1,), (1,)))
    mixing = mine - drift * later
    last = moved_own + growth * (moved_own - column) + dot(mixing, spans, ((1,), (0,)))
    last = last - jnp.sum(last, axis=1, keepdims=True) * (1.0 / total) + 1.0 / total

    settle("keep")
    for window, count in enumerate(WINDOWS):
        if count:
            settle(f"ensemble {window}")
    for x in range(rows):
        out[:, x] = dot(last, SF[:, x].reshape(total, cells), ((1,), (0,)))
    finish()


def on_device(ensemble, diffusivity, velocity, observed, obs_weight, noise):
    nd, nt, ny = (lax.axis_size(a) for a in ("dom", "tx", "ty"))
    mem, rows, cells = ensemble.shape
    total = mem * nd
    iters = noise.shape[0]
    cell_count = rows * nt * cells * ny
    step_size = total / (4.0 * cell_count)
    growth = step_size * (cell_count + 1) / total
    drift = step_size / total
    spread = math.sqrt(2.0 * step_size / total)
    f32 = functools.partial(pltpu.VMEM, dtype=jnp.float32)
    high = mem + COEFS
    half = mem // 2
    quads = nt * (ny // 2)
    scratch = [
        f32((rows + 4, high, cells)),
        f32((rows + 4, high, LANES)),
        f32((rows, high, LANES)),
        f32((rows, high, LANES)),
        f32((4, mem, LANES)),
        f32((rows + 2, mem, cells + LANES)),
        f32((rows, mem, cells)),
        f32((nd, mem, cells)),
        f32((nd, mem, cells)),
        f32((nd, rows, mem, cells)),
        f32((rows, cells)),
        f32((rows, cells)),
        f32((iters, mem, total)),
        f32((nd, mem, total)),
        f32((2 * nd, half, total)),
        f32((2 * nd, half, total)),
        f32((half, total)),
        f32((quads, half, total)),
        f32((half, total)),
        f32((2 * nd, half, total)),
        f32((nd, mem, total)),
        pltpu.SemaphoreType.DMA((8 + rows,)),
        pltpu.SemaphoreType.DMA((18,)),
        pltpu.SemaphoreType.DMA((8,)),
        pltpu.SemaphoreType.DMA((10,)),
    ]
    return pl.pallas_call(
        functools.partial(kernel, (nd, nt, ny, rows, mem, total), (growth, drift, spread)),
        out_shape=pltpu.VMEM(ensemble.shape, jnp.float32),
        in_specs=[pl.BlockSpec(memory_space=pltpu.HBM)] * 6,
        out_specs=pl.BlockSpec(memory_space=pltpu.VMEM),
        scratch_shapes=scratch,
        compiler_params=pltpu.CompilerParams(
            collective_id=0, has_side_effects=True, vmem_limit_bytes=63 * 2**20
        ),
        name="langevin",
    )(ensemble, diffusivity, velocity, observed, obs_weight, jnp.swapaxes(noise, 1, 2))


def solution(mesh):
    return jax.shard_map(
        on_device,
        mesh=mesh,
        in_specs=(
            P("dom", "tx", "ty"),
            P("tx", "ty"),
            P(None, "tx", "ty"),
            P("tx", "ty"),
            P("tx", "ty"),
            P(None, None, "dom"),
        ),
        out_specs=P("dom", "tx", "ty"),
        check_vma=False,
    )
```

```python
import functools
import itertools
import math

import jax
import jax.numpy as jnp
from jax import lax
from jax.experimental import pallas as pl
from jax.experimental.pallas import tpu as pltpu
from jax.sharding import PartitionSpec as P

NZ = 32
MESH = pl.DeviceIdType.MESH
LANES = 128
COEFS = 8


def dot(a, b, dims):
    return lax.dot_general(
        a,
        b,
        (dims, ((), ())),
        precision=lax.Precision.HIGHEST,
        preferred_element_type=jnp.float32,
    )


def step_row(here, west, east, coefs, tiles):
    lane = lax.broadcasted_iota(jnp.int32, (1, LANES), 1)
    depth = lane % NZ
    up = [pltpu.roll(tile, NZ, 1) for tile in here]
    down = [pltpu.roll(tile, LANES - NZ, 1) for tile in here]
    out = []
    for k in range(tiles):
        diffusion, vx, vy, vz = (coefs[k][i : i + 1] for i in range(4))
        centre = 1.0 - 6.0 * diffusion - vx - vy - vz
        south = jnp.where(lane < NZ, up[(k + 2) % 3], up[k])
        north = jnp.where(lane >= LANES - NZ, down[(k + 1) % 3], down[k])
        below = pltpu.roll(here[k], 1, 1)
        above = pltpu.roll(here[k], LANES - 1, 1)
        result = centre * here[k] + diffusion * (east[k] + north)
        result = result + (diffusion + vx) * west[k] + (diffusion + vy) * south
        result = result + jnp.where(depth > 0, diffusion + vz, 0.0) * below
        result = result + jnp.where(depth < NZ - 1, diffusion, 0.0) * above
        out.append(result)
    return out


def kernel(
    sizes, consts,
    ens, dif, vel, obs, wgt, noi, out,
    XB, TB, YL, YR, CN, LB, YB, SA, YA, SF, OV, WV, NV, NA, GP, RL, RB, AL, AB, GA, DV,
    load, send, hrecv, recv,
):
    nd, nt, ny, rows, mem, total = sizes
    growth, drift, spread = consts
    d, t, y = lax.axis_index("dom"), lax.axis_index("tx"), lax.axis_index("ty")
    chip_y, core = y // 2, lax.rem(y, 2)
    blk, quad = d * 2 + core, t * (ny // 2) + chip_y
    width = rows + 4

    def at(dd, tt, yy):
        return (lax.rem(d + dd, nd), lax.rem(t + tt, nt), lax.rem(y + yy, ny))

    nx, chips = nd // 2, ny // 2
    x, z = d // 2, lax.rem(d, 2)

    def hops(*pairs):
        return sum(min(step, size - step) * cost for step, size, cost in pairs)

    dc_peers = []
    for c, a, b in sorted(
        itertools.product((0, 1), range(nx), (0, 1)),
        key=lambda cab: -hops((cab[1], nx, 2), (cab[2], 2, 2), (cab[0], 2, 1)),
    )[:-1]:
        there = lax.rem(x + a, nx) * 2 + lax.rem(z + b, 2)
        dc_peers.append((there, t, chip_y * 2 + lax.rem(core + c, 2), c))
    dom_peers = [peer[:3] for peer in dc_peers if peer[3] == 0]
    dc_peers = [peer[:3] for peer in dc_peers]
    x_peers = [(lax.rem(x + a, nx) * 2 + z, t, y) for a in sorted(range(1, nx), key=lambda a: -hops((a, nx, 1)))]
    pair = (x * 2 + 1 - z, t, y)
    yt_peers = []
    for a, b in sorted(
        itertools.product(range(nt), range(chips)),
        key=lambda ab: -hops((ab[0], nt, 2), (ab[1], chips, 1)),
    )[:-1]:
        yt_peers.append((d, lax.rem(t + a, nt), lax.rem(chip_y + b, chips) * 2 + core))
    halo_peers = {}
    for a, b in itertools.product((-1, 0, 1), (-1, 0, 1)):
        if a or b:
            halo_peers[(a, b)] = at(0, a % nt, b % ny)

    barrier = pltpu.get_barrier_semaphore()
    greeted = [at(0, a % nt, b % ny) for a in (-1, 1) for b in (-2, -1, 1, 2, 0)] + dom_peers
    greeted += [at(0, 0, b % ny) for b in (-2, 2, -1, 1)]
    for peer in greeted:
        pl.semaphore_signal(barrier, inc=1, device_id=peer, device_id_type=MESH)

    pending = {}

    def settle(name):
        pending.pop(name)()

    def finish():
        for name in list(pending):
            settle(name)


    loads = [pltpu.make_async_copy(dif, XB.at[pl.ds(2, rows), mem], load.at[0])]
    for k in range(3):
        loads.append(
            pltpu.make_async_copy(vel.at[k], XB.at[pl.ds(2, rows), mem + 1 + k], load.at[1 + k])
        )
    for r in range(rows):
        loads.append(
            pltpu.make_async_copy(ens.at[:, r], XB.at[2 + r, pl.ds(0, mem)], load.at[4 + r])
        )
    for copy in loads:
        copy.start()
    extras = [
        pltpu.make_async_copy(src, dst, load.at[4 + rows + k])
        for k, (src, dst) in enumerate(((obs, OV), (wgt, WV), (noi, NV)))
    ]
    for copy in extras:
        copy.start()
    zero = jnp.zeros((1,) + TB.shape[1:], jnp.float32)
    TB[0:1] = zero
    TB[width - 1 : width] = zero
    for copy in loads + extras:
        copy.wait()

    pl.semaphore_wait(barrier, len(greeted))

    def remote(src, dst, ss, rs, peer):
        copy = pltpu.make_async_remote_copy(
            src_ref=src, dst_ref=dst, send_sem=ss, recv_sem=rs, device_id=peer, device_id_type=MESH
        )
        copy.start()
        return copy

    left, right = pl.ds(0, LANES), pl.ds(LANES, LANES)
    own, body = pl.ds(0, mem), pl.ds(2, rows)
    halos = []
    for i, (key, src, dst) in enumerate(
        (
            ((1, 0), XB.at[pl.ds(rows, 2)], XB.at[pl.ds(0, 2)]),
            ((-1, 0), XB.at[pl.ds(2, 2)], XB.at[pl.ds(rows + 2, 2)]),
            ((0, 1), XB.at[body, :, right], YL),
            ((0, -1), XB.at[body, :, left], YR),
            ((1, 1), XB.at[rows + 1, own, right], CN.at[0]),
            ((1, -1), XB.at[rows + 1, own, left], CN.at[1]),
            ((-1, 1), XB.at[2, own, right], CN.at[2]),
            ((-1, -1), XB.at[2, own, left], CN.at[3]),
        )
    ):
        halos.append(remote(src, dst, send.at[6 + i], hrecv.at[i], halo_peers[key]))
    for k, peer in enumerate(dom_peers):
        remote(XB.at[2 + peer[0], own], SA.at[d], send.at[0], recv.at[0], peer)
    for k, peer in enumerate(dom_peers):
        remote(NV.at[0], NA.at[d], send.at[1], recv.at[1], peer)

    def wait_all(name, ref, count, sem):
        def wait():
            part = ref.at[pl.ds(0, count)]
            pltpu.make_async_copy(part, part, sem).wait()

        pending[name] = wait

    def hand_out(name, slot, peers, sem):
        for peer in peers:
            src = XB.at[body, own] if slot is d else SF.at[slot]
            remote(src, SF.at[slot], send.at[14 + sem], recv.at[6 + sem], peer)
        wait_all(name, SF, len(peers), recv.at[6 + sem])
        wait_all(name + " sent", SF, len(peers), send.at[14 + sem])

    hand_out("near", d, x_peers, 0)
    keep = pltpu.make_async_copy(XB.at[body, own], SF.at[d], load.at[7 + rows])
    keep.start()
    pending['keep'] = keep.wait
    SA[d] = XB[2 + d, 0:mem]
    NA[d] = NV[0]

    def wait_halos():
        for copy in halos:
            copy.wait_recv()

    def sent_halos():
        for copy in halos:
            copy.wait_send()

    pending["halos"] = wait_halos
    pending["halos sent"] = sent_halos
    wait_all("members", SA, nd - 1, recv.at[0])
    wait_all("members sent", SA, nd - 1, send.at[0])
    wait_all("noise", NA, nd - 1, recv.at[1])
    wait_all("noise sent", NA, nd - 1, send.at[1])
    settle("halos")

    @pl.when(t == 0)
    def _():
        XB[0:2] = jnp.zeros((2,) + XB.shape[1:], jnp.float32)

    @pl.when(t == nt - 1)
    def _():
        XB[rows + 2 : rows + 4] = jnp.zeros((2,) + XB.shape[1:], jnp.float32)

    has_left = (y > 0).astype(jnp.float32)
    has_right = (y < ny - 1).astype(jnp.float32)
    has_west = (t > 0).astype(jnp.float32)
    has_east = (t < nt - 1).astype(jnp.float32)
    is_right = lax.broadcasted_iota(jnp.int32, (1, LANES), 1) < LANES // 2
    TB[2 : rows + 2] = jnp.where(is_right[None], YR[...] * has_right, YL[...] * has_left)
    TB[1, 0:mem] = jnp.where(is_right, CN[1] * has_right, CN[0] * has_left) * has_west
    TB[rows + 2, 0:mem] = jnp.where(is_right, CN[3] * has_right, CN[2] * has_left) * has_east
    TB[1, mem:] = zero[0, mem:]
    TB[rows + 2, mem:] = zero[0, mem:]

    def tiles_of(r):
        return [XB[r, 0:mem, 0:LANES], XB[r, 0:mem, LANES:], TB[r, 0:mem]]

    def first(r, carry):
        coefs = [XB[r, mem:, 0:LANES], XB[r, mem:, LANES:], TB[r, mem:]]
        found = step_row(tiles_of(r), tiles_of(r - 1), tiles_of(r + 1), coefs, 3)
        for k in range(3):
            LB[r - 1, :, k * LANES : (k + 1) * LANES] = found[k]
        return carry

    lax.fori_loop(1, rows + 3, first, 0)

    def second(r, carry):
        coefs = [XB[r + 2, mem:, 0:LANES], XB[r + 2, mem:, LANES:]]
        mid, before, after = (
            [LB[s, :, k * LANES : (k + 1) * LANES] for k in range(3)] for s in (r + 1, r, r + 2)
        )
        found = step_row(mid, before, after, coefs, 2)
        for k in range(2):
            YB[r, :, k * LANES : (k + 1) * LANES] = found[k]
        return carry

    lax.fori_loop(0, rows, second, 0)

    for peer in dom_peers:
        remote(YB.at[peer[0]], YA.at[d], send.at[2], recv.at[2], peer)
    YA[d] = YB[d]
    wait_all("images", YA, nd - 1, recv.at[2])
    wait_all("images sent", YA, nd - 1, send.at[2])
    settle("members")
    cells = SA.shape[2]
    state = SA[...].reshape(total, cells)
    anomaly = state - jnp.sum(state, axis=0, keepdims=True) * (1.0 / total)
    near = dot(state, anomaly, ((1,), (1,)))
    target, weight = OV[pl.ds(d, 1)], WV[pl.ds(d, 1)]
    settle("images")
    image = YA[...].reshape(total, cells)
    centred = weight * (image - jnp.sum(image, axis=0, keepdims=True) * (1.0 / total))
    gram = near + dot(image - target, centred, ((1,), (1,)))
    GP[...] = gram.reshape(GP.shape)

    for peer in dc_peers:
        theirs = peer[0] * 2 + lax.rem(peer[2], 2)
        remote(GP.at[theirs], RL.at[blk], send.at[3], recv.at[3], peer)
    RL[blk] = GP[blk]
    wait_all("parts", RL, 2 * nd - 1, recv.at[3])
    wait_all("parts sent", RL, 2 * nd - 1, send.at[3])
    hand_out("pair", d, [pair], 1)
    settle("parts")
    RB[...] = jnp.sum(RL[...], axis=0)
    for peer in yt_peers:
        remote(RB, AL.at[quad], send.at[4], recv.at[4], peer)
    AL[quad] = RB[...]
    wait_all("tiles", AL, len(yt_peers), recv.at[4])
    wait_all("tiles sent", AL, len(yt_peers), send.at[4])
    settle("pair")
    hand_out("far", pair[0], x_peers, 2)
    settle("tiles")
    AB[...] = jnp.sum(AL[...], axis=0)
    for peer in dc_peers:
        remote(AB, GA.at[blk], send.at[5], recv.at[5], peer)
    GA[blk] = AB[...]
    wait_all("blocks", GA, 2 * nd - 1, recv.at[5])
    wait_all("blocks sent", GA, 2 * nd - 1, send.at[5])
    settle("noise")
    mine = spread * NV[1]
    settle("blocks")

    gram = GA[...].reshape(total, total)
    noise = NA[...].reshape(total, total)
    eye = (
        lax.broadcasted_iota(jnp.int32, (total, total), 0)
        == lax.broadcasted_iota(jnp.int32, (total, total), 1)
    ).astype(jnp.float32)
    moved = (1.0 + growth) * eye + (spread * noise - drift * gram)
    DV[...] = moved.reshape(DV.shape)
    column = jnp.sum(moved, axis=0, keepdims=True) * (1.0 / total)
    spans = moved - column
    moved_own = DV[d]
    weights = moved_own - jnp.sum(moved_own, axis=1, keepdims=True) * (1.0 / total) + 1.0 / total
    later = dot(dot(weights, gram, ((1,), (0,))), spans, ((1,), (1,)))
    mixing = mine - drift * later
    last = moved_own + growth * (moved_own - column) + dot(mixing, spans, ((1,), (0,)))
    last = last - jnp.sum(last, axis=1, keepdims=True) * (1.0 / total) + 1.0 / total

    settle("keep")
    settle("near")
    settle("far")
    for r in range(rows):
        out[:, r] = dot(last, SF[:, r].reshape(total, cells), ((1,), (0,)))
    finish()


def on_device(ensemble, diffusivity, velocity, observed, obs_weight, noise):
    nd, nt, ny = (lax.axis_size(a) for a in ("dom", "tx", "ty"))
    mem, rows, cells = ensemble.shape
    total = mem * nd
    iters = noise.shape[0]
    cell_count = rows * nt * cells * ny
    step_size = total / (4.0 * cell_count)
    growth = step_size * (cell_count + 1) / total
    drift = step_size / total
    spread = math.sqrt(2.0 * step_size / total)
    f32 = functools.partial(pltpu.VMEM, dtype=jnp.float32)
    high = mem + COEFS
    half = mem // 2
    quads = nt * (ny // 2)
    scratch = [
        f32((rows + 4, high, cells)),
        f32((rows + 4, high, LANES)),
        f32((rows, high, LANES)),
        f32((rows, high, LANES)),
        f32((4, mem, LANES)),
        f32((rows + 2, mem, cells + LANES)),
        f32((rows, mem, cells)),
        f32((nd, mem, cells)),
        f32((nd, mem, cells)),
        f32((nd, rows, mem, cells)),
        f32((rows, cells)),
        f32((rows, cells)),
        f32((iters, mem, total)),
        f32((nd, mem, total)),
        f32((2 * nd, half, total)),
        f32((2 * nd, half, total)),
        f32((half, total)),
        f32((quads, half, total)),
        f32((half, total)),
        f32((2 * nd, half, total)),
        f32((nd, mem, total)),
        pltpu.SemaphoreType.DMA((8 + rows,)),
        pltpu.SemaphoreType.DMA((18,)),
        pltpu.SemaphoreType.DMA((8,)),
        pltpu.SemaphoreType.DMA((10,)),
    ]
    return pl.pallas_call(
        functools.partial(kernel, (nd, nt, ny, rows, mem, total), (growth, drift, spread)),
        out_shape=pltpu.VMEM(ensemble.shape, jnp.float32),
        in_specs=[pl.BlockSpec(memory_space=pltpu.HBM)] * 6,
        out_specs=pl.BlockSpec(memory_space=pltpu.VMEM),
        scratch_shapes=scratch,
        compiler_params=pltpu.CompilerParams(
            collective_id=0, has_side_effects=True, vmem_limit_bytes=63 * 2**20
        ),
        name="langevin",
    )(ensemble, diffusivity, velocity, observed, obs_weight, jnp.swapaxes(noise, 1, 2))


def solution(mesh):
    return jax.shard_map(
        on_device,
        mesh=mesh,
        in_specs=(
            P("dom", "tx", "ty"),
            P("tx", "ty"),
            P(None, "tx", "ty"),
            P("tx", "ty"),
            P("tx", "ty"),
            P(None, None, "dom"),
        ),
        out_specs=P("dom", "tx", "ty"),
        check_vma=False,
    )
```

```python
import functools
import itertools
import math

import jax
import jax.numpy as jnp
from jax import lax
from jax.experimental import pallas as pl
from jax.experimental.pallas import tpu as pltpu
from jax.sharding import PartitionSpec as P

NZ = 32
MESH = pl.DeviceIdType.MESH
LANES = 128


def dot(a, b, dims):
    return lax.dot_general(
        a,
        b,
        (dims, ((), ())),
        precision=lax.Precision.HIGHEST,
        preferred_element_type=jnp.float32,
    )


def step_row(here, west, east, coefs, tiles):
    lane = lax.broadcasted_iota(jnp.int32, (1, LANES), 1)
    depth = lane % NZ
    up = [pltpu.roll(tile, NZ, 1) for tile in here]
    down = [pltpu.roll(tile, LANES - NZ, 1) for tile in here]
    out = []
    for k in range(tiles):
        diffusion, vx, vy, vz = (coefs[k][i : i + 1] for i in range(4))
        centre = 1.0 - 6.0 * diffusion - vx - vy - vz
        south = jnp.where(lane < NZ, up[(k + 2) % 3], up[k])
        north = jnp.where(lane >= LANES - NZ, down[(k + 1) % 3], down[k])
        below = pltpu.roll(here[k], 1, 1)
        above = pltpu.roll(here[k], LANES - 1, 1)
        result = centre * here[k] + diffusion * (east[k] + north)
        result = result + (diffusion + vx) * west[k] + (diffusion + vy) * south
        result = result + jnp.where(depth > 0, diffusion + vz, 0.0) * below
        result = result + jnp.where(depth < NZ - 1, diffusion, 0.0) * above
        out.append(result)
    return out


def kernel(
    sizes, consts,
    ens, dif, vel, obs, wgt, noi, out,
    XB, TB, CB, TC, YL, YR, CL, CR, CS, CN, LB, YB, SA, YA, SF, OV, WV, NV, NA, GP, RL, RB, AL, AB, GA, DV,
    load, send, hrecv, recv,
):
    nd, nt, ny, rows, mem, total = sizes
    growth, drift, spread = consts
    d, t, y = lax.axis_index("dom"), lax.axis_index("tx"), lax.axis_index("ty")
    chip_y, core = y // 2, lax.rem(y, 2)
    blk, quad = d * 2 + core, t * (ny // 2) + chip_y
    width = rows + 4

    def at(dd, tt, yy):
        return (lax.rem(d + dd, nd), lax.rem(t + tt, nt), lax.rem(y + yy, ny))

    nx, chips = nd // 2, ny // 2
    x, z = d // 2, lax.rem(d, 2)

    def hops(*pairs):
        return sum(min(step, size - step) * cost for step, size, cost in pairs)

    dc_peers = []
    for c, a, b in sorted(
        itertools.product((0, 1), range(nx), (0, 1)),
        key=lambda cab: -hops((cab[1], nx, 2), (cab[2], 2, 2), (cab[0], 2, 1)),
    )[:-1]:
        there = lax.rem(x + a, nx) * 2 + lax.rem(z + b, 2)
        dc_peers.append((there, t, chip_y * 2 + lax.rem(core + c, 2), c))
    dom_peers = [peer[:3] for peer in dc_peers if peer[3] == 0]
    dc_peers = [peer[:3] for peer in dc_peers]
    x_peers = [(lax.rem(x + a, nx) * 2 + z, t, y) for a in sorted(range(1, nx), key=lambda a: -hops((a, nx, 1)))]
    pair = (x * 2 + 1 - z, t, y)
    yt_peers = []
    for a, b in sorted(
        itertools.product(range(nt), range(chips)),
        key=lambda ab: -hops((ab[0], nt, 2), (ab[1], chips, 1)),
    )[:-1]:
        yt_peers.append((d, lax.rem(t + a, nt), lax.rem(chip_y + b, chips) * 2 + core))
    halo_peers = {}
    for a, b in itertools.product((-1, 0, 1), (-1, 0, 1)):
        if a or b:
            halo_peers[(a, b)] = at(0, a % nt, b % ny)

    barrier = pltpu.get_barrier_semaphore()
    greeted = [at(0, a % nt, b % ny) for a in (-1, 1) for b in (-2, -1, 1, 2, 0)] + dom_peers
    greeted += [at(0, 0, b % ny) for b in (-2, 2, -1, 1)]
    for peer in greeted:
        pl.semaphore_signal(barrier, inc=1, device_id=peer, device_id_type=MESH)

    pending = {}

    def settle(name):
        pending.pop(name)()

    def finish():
        for name in list(pending):
            settle(name)


    loads = []
    for k, field in enumerate((dif, vel.at[0], vel.at[1], vel.at[2])):
        for half in range(2):
            loads.append(
                pltpu.make_async_copy(
                    field.at[:, pl.ds(half * LANES, LANES)],
                    CB.at[pl.ds(2, rows), half * 4 + k],
                    load.at[2 * k + half],
                )
            )
    for r in range(rows):
        loads.append(
            pltpu.make_async_copy(ens.at[:, r], XB.at[2 + r], load.at[8 + r])
        )
    for copy in loads:
        copy.start()
    extras = [
        pltpu.make_async_copy(src, dst, load.at[8 + rows + k])
        for k, (src, dst) in enumerate(((obs, OV), (wgt, WV), (noi, NV)))
    ]
    for copy in extras:
        copy.start()
    for r in (0, width - 1):
        TB[r] = jnp.zeros(TB.shape[1:], jnp.float32)
    for r in (1, width - 2):
        TC[r] = jnp.zeros(TC.shape[1:], jnp.float32)
    for copy in loads + extras:
        copy.wait()

    pl.semaphore_wait(barrier, len(greeted))

    def remote(src, dst, ss, rs, peer):
        copy = pltpu.make_async_remote_copy(
            src_ref=src, dst_ref=dst, send_sem=ss, recv_sem=rs, device_id=peer, device_id_type=MESH
        )
        copy.start()
        return copy

    left, right, body = pl.ds(0, LANES), pl.ds(LANES, LANES), pl.ds(2, rows)
    lane = lax.broadcasted_iota(jnp.int32, (1, LANES), 1)
    low, half = lane < LANES // 2, mem // 2
    for i, r in enumerate((rows + 1, 2)):
        east_end, west_end = XB[r, :, LANES:], XB[r, :, 0:LANES]
        CS[2 * i] = jnp.where(low, pltpu.roll(east_end[:half], LANES // 2, 1), east_end[half:])
        CS[2 * i + 1] = jnp.where(low, west_end[:half], pltpu.roll(west_end[half:], LANES // 2, 1))
    halos = []
    for i, (key, src, dst) in enumerate(
        (
            ((1, 1), CS.at[0], CN.at[0]),
            ((1, -1), CS.at[1], CN.at[1]),
            ((-1, 1), CS.at[2], CN.at[2]),
            ((-1, -1), CS.at[3], CN.at[3]),
            ((1, 0), XB.at[pl.ds(rows, 2)], XB.at[pl.ds(0, 2)]),
            ((-1, 0), XB.at[pl.ds(2, 2)], XB.at[pl.ds(rows + 2, 2)]),
            ((1, 0), CB.at[rows + 1], CB.at[1]),
            ((-1, 0), CB.at[2], CB.at[rows + 2]),
            ((0, 1), XB.at[body, :, right], YL),
            ((0, -1), XB.at[body, :, left], YR),
            ((0, 1), CB.at[body], CL),
            ((0, -1), CB.at[body], CR),
        )
    ):
        halos.append(remote(src, dst, send.at[12 + i], hrecv.at[i], halo_peers[key]))
    for k, peer in enumerate(dom_peers):
        remote(XB.at[2 + peer[0]], SA.at[d], send.at[0], recv.at[0], peer)
    for k, peer in enumerate(dom_peers):
        remote(NV.at[0], NA.at[d], send.at[1], recv.at[1], peer)

    def wait_all(name, ref, count, sem):
        def wait():
            part = ref.at[pl.ds(0, count)]
            pltpu.make_async_copy(part, part, sem).wait()

        pending[name] = wait

    def hand_out(name, slot, peers, sem, part=(0, rows)):
        part = pl.ds(part[0], part[1] - part[0])
        for peer in peers:
            src = XB.at[pl.ds(2 + part.start, part.size)] if slot is d else SF.at[slot, part]
            remote(src, SF.at[slot, part], send.at[6 + sem], recv.at[6 + sem], peer)
        if peers:
            slots = SF.at[:, part]
            wait_all(name, slots, len(peers), recv.at[6 + sem])
            wait_all(name + " sent", slots, len(peers), send.at[6 + sem])

    hand_out("near0", d, x_peers, 0, (0, rows * 3 // 4))
    keep = pltpu.make_async_copy(XB.at[body], SF.at[d], load.at[11 + rows])
    keep.start()
    pending['keep'] = keep.wait
    SA[d] = XB[2 + d]
    NA[d] = NV[0]

    def wait_halos():
        for copy in halos:
            copy.wait_recv()

    def sent_halos():
        for copy in halos:
            copy.wait_send()

    pending["halos"] = wait_halos
    pending["halos sent"] = sent_halos
    wait_all("members", SA, nd - 1, recv.at[0])
    wait_all("members sent", SA, nd - 1, send.at[0])
    wait_all("noise", NA, nd - 1, recv.at[1])
    wait_all("noise sent", NA, nd - 1, send.at[1])
    settle("halos")

    @pl.when(t == 0)
    def _():
        XB[0:2] = jnp.zeros((2,) + XB.shape[1:], jnp.float32)
        CB[1] = jnp.zeros(CB.shape[1:], jnp.float32)

    @pl.when(t == nt - 1)
    def _():
        XB[rows + 2 : rows + 4] = jnp.zeros((2,) + XB.shape[1:], jnp.float32)
        CB[rows + 2] = jnp.zeros(CB.shape[1:], jnp.float32)

    has_left = (y > 0).astype(jnp.float32)
    has_right = (y < ny - 1).astype(jnp.float32)
    has_west = (t > 0).astype(jnp.float32)
    has_east = (t < nt - 1).astype(jnp.float32)
    TB[2 : rows + 2] = jnp.where(low[None], YR[...] * has_right, YL[...] * has_left)
    TC[2 : rows + 2] = jnp.where(low[None], CR[:, 0:4] * has_right, CL[:, 4:8] * has_left)
    for i, (r, has) in enumerate(((1, has_west), (rows + 2, has_east))):
        west_end, east_end = CN[2 * i] * (has_left * has), CN[2 * i + 1] * (has_right * has)
        TB[r, :half] = jnp.where(low, east_end, pltpu.roll(west_end, LANES // 2, 1))
        TB[r, half:] = jnp.where(low, pltpu.roll(east_end, LANES // 2, 1), west_end)

    def tiles_of(r):
        return [XB[r, :, 0:LANES], XB[r, :, LANES:], TB[r]]

    def first(r, carry):
        coefs = [CB[r, 0:4], CB[r, 4:8], TC[r]]
        found = step_row(tiles_of(r), tiles_of(r - 1), tiles_of(r + 1), coefs, 3)
        for k in range(3):
            LB[r - 1, :, k * LANES : (k + 1) * LANES] = found[k]
        return carry

    lax.fori_loop(1, rows + 3, first, 0, unroll=5)

    def second(r, carry):
        coefs = [CB[r + 2, 0:4], CB[r + 2, 4:8]]
        mid, before, after = (
            [LB[s, :, k * LANES : (k + 1) * LANES] for k in range(3)] for s in (r + 1, r, r + 2)
        )
        found = step_row(mid, before, after, coefs, 2)
        for k in range(2):
            YB[r, :, k * LANES : (k + 1) * LANES] = found[k]
        return carry

    lax.fori_loop(0, rows, second, 0, unroll=4)

    for peer in dom_peers:
        remote(YB.at[peer[0]], YA.at[d], send.at[2], recv.at[2], peer)
    YA[d] = YB[d]
    wait_all("images", YA, nd - 1, recv.at[2])
    wait_all("images sent", YA, nd - 1, send.at[2])
    settle("members")
    cells = SA.shape[2]
    state = SA[...].reshape(total, cells)
    anomaly = state - jnp.sum(state, axis=0, keepdims=True) * (1.0 / total)
    near = dot(state, anomaly, ((1,), (1,)))
    target, weight = OV[pl.ds(d, 1)], WV[pl.ds(d, 1)]
    settle("images")
    image = YA[...].reshape(total, cells)
    centred = weight * (image - jnp.sum(image, axis=0, keepdims=True) * (1.0 / total))
    gram = near + dot(image - target, centred, ((1,), (1,)))
    GP[...] = gram.reshape(GP.shape)

    for peer in dc_peers:
        theirs = peer[0] * 2 + lax.rem(peer[2], 2)
        remote(GP.at[theirs], RL.at[blk], send.at[3], recv.at[3], peer)
    RL[blk] = GP[blk]
    wait_all("parts", RL, 2 * nd - 1, recv.at[3])
    wait_all("parts sent", RL, 2 * nd - 1, send.at[3])
    hand_out("pair", d, [pair], 1)
    hand_out("near1", d, x_peers, 3, (rows * 3 // 4, rows))
    settle("parts")
    RB[...] = jnp.sum(RL[...], axis=0)
    for peer in yt_peers:
        remote(RB, AL.at[quad], send.at[4], recv.at[4], peer)
    AL[quad] = RB[...]
    wait_all("tiles", AL, len(yt_peers), recv.at[4])
    wait_all("tiles sent", AL, len(yt_peers), send.at[4])
    settle("pair")
    hand_out("far", pair[0], x_peers, 2)
    settle("tiles")
    AB[...] = jnp.sum(AL[...], axis=0)
    for peer in dc_peers:
        remote(AB, GA.at[blk], send.at[5], recv.at[5], peer)
    GA[blk] = AB[...]
    wait_all("blocks", GA, 2 * nd - 1, recv.at[5])
    wait_all("blocks sent", GA, 2 * nd - 1, send.at[5])
    settle("noise")
    mine = spread * NV[1]
    settle("blocks")

    gram = GA[...].reshape(total, total)
    noise = NA[...].reshape(total, total)
    eye = (
        lax.broadcasted_iota(jnp.int32, (total, total), 0)
        == lax.broadcasted_iota(jnp.int32, (total, total), 1)
    ).astype(jnp.float32)
    moved = (1.0 + growth) * eye + (spread * noise - drift * gram)
    DV[...] = moved.reshape(DV.shape)
    column = jnp.sum(moved, axis=0, keepdims=True) * (1.0 / total)
    spans = moved - column
    moved_own = DV[d]
    weights = moved_own - jnp.sum(moved_own, axis=1, keepdims=True) * (1.0 / total) + 1.0 / total
    later = dot(dot(weights, gram, ((1,), (0,))), spans, ((1,), (1,)))
    mixing = mine - drift * later
    last = moved_own + growth * (moved_own - column) + dot(mixing, spans, ((1,), (0,)))
    last = last - jnp.sum(last, axis=1, keepdims=True) * (1.0 / total) + 1.0 / total

    settle("keep")
    settle("near0")
    settle("near1")
    settle("far")
    for r in range(rows):
        out[:, r] = dot(last, SF[:, r].reshape(total, cells), ((1,), (0,)))
    finish()


def on_device(ensemble, diffusivity, velocity, observed, obs_weight, noise):
    nd, nt, ny = (lax.axis_size(a) for a in ("dom", "tx", "ty"))
    mem, rows, cells = ensemble.shape
    total = mem * nd
    iters = noise.shape[0]
    cell_count = rows * nt * cells * ny
    step_size = total / (4.0 * cell_count)
    growth = step_size * (cell_count + 1) / total
    drift = step_size / total
    spread = math.sqrt(2.0 * step_size / total)
    f32 = functools.partial(pltpu.VMEM, dtype=jnp.float32)
    half = mem // 2
    quads = nt * (ny // 2)
    scratch = [
        f32((rows + 4, mem, cells)),
        f32((rows + 4, mem, LANES)),
        f32((rows + 4, 8, LANES)),
        f32((rows + 4, 4, LANES)),
        f32((rows, mem, LANES)),
        f32((rows, mem, LANES)),
        f32((rows, 8, LANES)),
        f32((rows, 8, LANES)),
        f32((4, mem // 2, LANES)),
        f32((4, mem // 2, LANES)),
        f32((rows + 2, mem, cells + LANES)),
        f32((rows, mem, cells)),
        f32((nd, mem, cells)),
        f32((nd, mem, cells)),
        f32((nd, rows, mem, cells)),
        f32((rows, cells)),
        f32((rows, cells)),
        f32((iters, mem, total)),
        f32((nd, mem, total)),
        f32((2 * nd, half, total)),
        f32((2 * nd, half, total)),
        f32((half, total)),
        f32((quads, half, total)),
        f32((half, total)),
        f32((2 * nd, half, total)),
        f32((nd, mem, total)),
        pltpu.SemaphoreType.DMA((12 + rows,)),
        pltpu.SemaphoreType.DMA((24,)),
        pltpu.SemaphoreType.DMA((12,)),
        pltpu.SemaphoreType.DMA((12,)),
    ]
    return pl.pallas_call(
        functools.partial(kernel, (nd, nt, ny, rows, mem, total), (growth, drift, spread)),
        out_shape=pltpu.VMEM(ensemble.shape, jnp.float32),
        in_specs=[pl.BlockSpec(memory_space=pltpu.HBM)] * 6,
        out_specs=pl.BlockSpec(memory_space=pltpu.VMEM),
        scratch_shapes=scratch,
        compiler_params=pltpu.CompilerParams(
            collective_id=0, has_side_effects=True, vmem_limit_bytes=63 * 2**20
        ),
        name="langevin",
    )(ensemble, diffusivity, velocity, observed, obs_weight, jnp.swapaxes(noise, 1, 2))


def solution(mesh):
    return jax.shard_map(
        on_device,
        mesh=mesh,
        in_specs=(
            P("dom", "tx", "ty"),
            P("tx", "ty"),
            P(None, "tx", "ty"),
            P("tx", "ty"),
            P("tx", "ty"),
            P(None, None, "dom"),
        ),
        out_specs=P("dom", "tx", "ty"),
        check_vma=False,
    )
```
